32 devices in a mesh: groups: 2 (over x), tensor: 16 (over z, y, core).
Axes of the slice: x: 2, y: 2, z: 4, core: 2. Of those that a mesh axis runs over, the one named last changes fastest.
Arguments:
- tokens: bfloat16 [2048, 8192], P(('groups', 'tensor')), parts along dimension 0, may hold values from -6 to 6
- gate_weight: bfloat16 [8192, 28672], P(None, 'tensor'), may hold values from -0.0625 to 0.0625
- adapter_shrink: bfloat16 [32, 8192, 64], P(('groups', 'tensor')), parts along dimension 0, may hold values from -0.0625 to 0.0625
- adapter_expand: bfloat16 [32, 64, 28672], P(('groups', 'tensor')), parts along dimension 0, may hold values from -0.75 to 0.75
- adapter_blocks: int32 [32], P('groups'), parts along dimension 0, may hold values from 1 to 4, 32 in all
- adapter_position: int32 [32], P('groups'), parts along dimension 0, may hold values from 0 to 15, each once
Outputs:
- projected: bfloat16 [2048, 28672], P('groups', 'tensor'), parts along dimension 0
The draws below stay inside these ranges and needn't reach their ends.
There are 2 independent parts, one for each index of `groups`. The reference program is written for one: setup_inputs(seed, part) draws one part's arguments, and reference() takes and returns one part's arrays. A program takes and returns all parts, laid end to end along the dimension named above; an argument that names none is the same for every part. Nothing has to cross between parts.
Inputs may be any that keep to these rules, and one draw needn't show every extreme that they name: Adapter k serves the 32-row blocks that follow those of adapters 0 to k-1, adapter_blocks[k] of them; some adapter serves exactly 4. Each storage position holds exactly one adapter; adapter k is stored on the device of index adapter_position[k] along tensor.
All inputs are finite; a program needn't handle non-finite values.
Results may differ from the reference program's by a relative error of at most 0.005.
Values may be sent and summed in bfloat16 or wider, within the bound.
No kernel may reach another device: no remote copies, remote signals or barrier semaphores. Data moves between devices by JAX's collectives and lax.ppermute only.
A program may use at most 192 MiB of HBM per device.

```python
import math
import jax
import jax.numpy as jnp
import numpy as np
from jax import lax

MODEL_WIDTH = 8192
HIDDEN_UNITS = 28672
ADAPTER_RANK = 64
BLOCK = 32
GROUP_ROWS = 1024
NBLK = 32
GROUP_ADAPTERS = 16
MOST = 4


def steps_of(stream_key, extent, shards, least, top_value):
    loudness = 1.0
    for dim, parts in shards:
        steps = jax.random.uniform(jax.random.fold_in(jax.random.fold_in(stream_key, 6), dim), (parts,), jnp.float32, least / len(shards), top_value / len(shards))
        loudness = loudness * jnp.repeat(jnp.exp(steps), extent[dim] // parts).reshape((-1,) + (1,) * (len(extent) - 1 - dim))
    return loudness


def split_up(count, total, most, lean):
    weights = [(1 << 20) // math.isqrt(rank ** lean) + 1 for rank in range(2, count + 1)]
    rest, holding = total - most - (count - 1), [1] * (count - 1)
    while rest > 0:
        movable = [i for i in range(count - 1) if holding[i] < most]
        whole, remaining = sum([weights[i] for i in movable]), rest
        for i in movable:
            more = min(most - holding[i], max(1, remaining * weights[i] // whole), rest)
            holding[i] = holding[i] + more
            rest = rest - more
    return np.array([most] + holding)


def ragged(rng, number_of, total, bound, skew):
    if number_of == 2:
        one = jax.random.randint(rng, (), max(1, total - bound), min(bound, total - 1) + 1)
        return jnp.stack([one, total - one])
    tallies = jnp.asarray(split_up(number_of, total, bound, skew), jnp.int32)
    couples = (number_of - 1) // 2
    giver, sink = tallies[1:1 + 2 * couples:2], tallies[2:2 + 2 * couples:2]
    room = jnp.minimum(giver - 1, bound - sink)
    moved = jax.random.randint(jax.random.fold_in(rng, 1), (couples,), 0, 1 << 20) % (room + 1)
    tallies = tallies.at[1:1 + 2 * couples:2].set(giver - moved).at[2:2 + 2 * couples:2].set(sink + moved)
    return tallies[jax.random.permutation(jax.random.fold_in(rng, 2), number_of)]


def scatter_about(stream_key, dims, spread, bound, pieces=(), kind=jnp.bfloat16):
    level = steps_of(stream_key, dims, pieces, -0.22, 0.18) if pieces else 1.0
    drawn = jax.random.normal(stream_key, dims, jnp.float32) * spread * level
    return jnp.minimum(jnp.maximum(drawn, -bound), bound).astype(kind)


def setup_inputs(seed: int = 0, part: int = 0) -> dict:
    key_list = jax.random.split(jax.random.key(seed), 7)
    own_keys = jax.random.split(jax.random.fold_in(key_list[6], part), 7)
    return {
        "tokens": scatter_about(own_keys[0], (GROUP_ROWS, MODEL_WIDTH), 1.0, 6.0, ((0, 16),)),
        "gate_weight": scatter_about(key_list[1], (MODEL_WIDTH, HIDDEN_UNITS), MODEL_WIDTH ** -0.5, 0.0625, ((1, 16),)),
        "adapter_shrink": scatter_about(own_keys[2], (GROUP_ADAPTERS, MODEL_WIDTH, ADAPTER_RANK), MODEL_WIDTH ** -0.5, 0.0625, ((0, 16),)),
        "adapter_expand": scatter_about(own_keys[3], (GROUP_ADAPTERS, ADAPTER_RANK, HIDDEN_UNITS), ADAPTER_RANK ** -0.5, 0.75, ((0, 16),)),
        "adapter_blocks": ragged(own_keys[4], GROUP_ADAPTERS, NBLK, MOST, 2).astype(jnp.int32),
        "adapter_position": jax.random.permutation(own_keys[5], GROUP_ADAPTERS).astype(jnp.int32),
    }


def reference(tokens, gate_weight, adapter_shrink, adapter_expand, adapter_blocks, adapter_position):
    seg_ends = jnp.cumsum(adapter_blocks).astype(jnp.int32)
    blocks = jnp.arange(NBLK, dtype=jnp.int32)
    block_adapter = jnp.sum((blocks[:, None] >= seg_ends[None, :]).astype(jnp.int32), axis=1).astype(jnp.int32)
    block_position = adapter_position[block_adapter].astype(jnp.int32)
    base_output = jnp.dot(tokens, gate_weight, preferred_element_type=jnp.float32)
    grouped_rows = tokens.reshape(NBLK, BLOCK, MODEL_WIDTH)

    def single_block(operands):
        rows_here, position_local = operands
        shrunk_rows = lax.dynamic_index_in_dim(adapter_shrink, position_local, 0, keepdims=False)
        expand_output = lax.dynamic_index_in_dim(adapter_expand, position_local, 0, keepdims=False)
        shrink = jnp.dot(rows_here, shrunk_rows, preferred_element_type=jnp.float32).astype(jnp.bfloat16)
        return jnp.dot(shrink, expand_output, preferred_element_type=jnp.float32).astype(jnp.bfloat16)

    adapter_output = lax.map(single_block, (grouped_rows, block_position)).reshape(GROUP_ROWS, HIDDEN_UNITS)
    adapter_output = lax.optimization_barrier(adapter_output)
    return (base_output + adapter_output.astype(jnp.float32)).astype(jnp.bfloat16)
```

```python
import functools

import jax
import jax.numpy as jnp
from jax import lax
from jax.experimental import pallas as pl
from jax.experimental.pallas import tpu as pltpu
from jax.sharding import PartitionSpec as P

BLOCK = 32
MOST = 4
AXIS = "tensor"
VMEM_LIMIT = 56 * 1024 * 1024
ANY = pl.BlockSpec(memory_space=pl.ANY)


def tie(values, after):
    count = len(values)

    def body(*refs):
        del refs

    return pl.pallas_call(
        body,
        out_shape=[jax.ShapeDtypeStruct(v.shape, v.dtype) for v in values],
        in_specs=[ANY] * (count + len(after)),
        out_specs=[ANY] * count,
        input_output_aliases={i: i for i in range(count)},
        name="tie",
    )(*values, *after)


def plane_kernel(pieces, fill, scalars, *refs):
    sources = refs[:pieces]
    weight, shrink_t = refs[pieces : pieces + 2]
    out, shrunk, rows, sem = refs[-4:]

    @pl.when(pl.program_id(0) == 0)
    def _():
        fill(scalars, sources, rows, sem)
        s = lax.dot_general(
            rows[...], shrink_t[...], (((1,), (1,)), ((), ())), preferred_element_type=jnp.float32
        ).astype(shrunk.dtype)
        shrunk[...] = jnp.concatenate([s, jnp.zeros_like(s)], axis=1)

    out[...] = jnp.dot(rows[...], weight[...], preferred_element_type=jnp.float32)


def plane_matmul(fill, scalars, sources, weight, shrink_t, held, total_rows, plane_rows, tile=256):
    depth, columns = weight.shape
    rank = shrink_t.shape[0]
    pieces = len(sources)
    aliases = {} if held is None else {1 + pieces + 2: 0, 1 + pieces + 3: 1}
    extra = () if held is None else tuple(held)
    while columns % tile:
        tile //= 2
    return pl.pallas_call(
        functools.partial(plane_kernel, pieces, fill),
        out_shape=[
            jax.ShapeDtypeStruct((total_rows, columns), jnp.float32),
            jax.ShapeDtypeStruct((total_rows, 2 * rank), jnp.bfloat16),
        ],
        grid_spec=pltpu.PrefetchScalarGridSpec(
            num_scalar_prefetch=1,
            grid=(columns // tile,),
            in_specs=[ANY] * pieces
            + [
                pl.BlockSpec((depth, tile), lambda n, s: (0, n)),
                pl.BlockSpec((rank, depth), lambda n, s: (0, 0)),
            ]
            + [ANY] * len(extra),
            out_specs=[
                pl.BlockSpec((plane_rows, tile), lambda n, s: (s[0], n)),
                pl.BlockSpec((plane_rows, 2 * rank), lambda n, s: (s[0], 0)),
            ],
            scratch_shapes=[pltpu.VMEM((plane_rows, depth), jnp.bfloat16), pltpu.SemaphoreType.DMA((2,))],
        ),
        input_output_aliases=aliases,
        compiler_params=pltpu.CompilerParams(vmem_limit_bytes=VMEM_LIMIT),
        cost_estimate=pl.CostEstimate(
            flops=2 * plane_rows * depth * columns,
            bytes_accessed=2 * depth * columns + 2 * plane_rows * depth + 4 * plane_rows * columns,
            transcendentals=0,
        ),
        name="plane",
    )(scalars, *sources, weight, shrink_t, *extra)


def fill_own(shard, scalars, sources, rows, sem):
    chip, across, across_other = sources
    y, core = scalars[1], scalars[2]
    other = (1 - y) * 2 * shard
    first = pltpu.make_async_copy(chip, rows.at[pl.ds(pl.multiple_of(y * 2 * shard, 2 * shard), 2 * shard)], sem.at[0])
    first.start()
    first.wait()
    second = pltpu.make_async_copy(
        across, rows.at[pl.ds(pl.multiple_of(other + core * shard, shard), shard)], sem.at[0]
    )
    third = pltpu.make_async_copy(
        across_other, rows.at[pl.ds(pl.multiple_of(other + (1 - core) * shard, shard), shard)], sem.at[1]
    )
    second.start()
    third.start()
    second.wait()
    third.wait()


def fill_far(shard, scalars, sources, rows, sem):
    y, chosen = scalars[1], scalars[3]
    mine = pl.ds(pl.multiple_of(y * 2 * shard, 2 * shard), 2 * shard)
    others = pl.ds(pl.multiple_of((1 - y) * 2 * shard, 2 * shard), 2 * shard)
    for i in range(len(sources) // 2):

        @pl.when(chosen == i)
        def _():
            first = pltpu.make_async_copy(sources[2 * i], rows.at[mine], sem.at[0])
            second = pltpu.make_async_copy(sources[2 * i + 1], rows.at[others], sem.at[1])
            first.start()
            second.start()
            first.wait()
            second.wait()


def last_kernel(slots, rank, begins, base, shrunk, expand, out, spread):
    capacity = shrunk.shape[1]

    @pl.when(pl.program_id(0) == 0)
    def _():
        spread[...] = jnp.zeros_like(spread)
        for s in range(slots):
            rows = pl.ds(pl.multiple_of(begins[s], BLOCK), capacity)
            spread[rows, s * rank : (s + 1) * rank] = shrunk[s, :, :rank]

    lora = jnp.dot(spread[...], expand[...], preferred_element_type=jnp.float32).astype(jnp.bfloat16)
    out[...] = (base[...] + lora.astype(jnp.float32)).astype(jnp.bfloat16)


def last(begins, base, shrunk, expand, rank, tile=256):
    total_rows, columns = base.shape
    slots, capacity, wide = shrunk.shape
    while columns % tile:
        tile //= 2
    return pl.pallas_call(
        functools.partial(last_kernel, slots, rank),
        out_shape=jax.ShapeDtypeStruct((total_rows, columns), jnp.bfloat16),
        grid_spec=pltpu.PrefetchScalarGridSpec(
            num_scalar_prefetch=1,
            grid=(columns // tile,),
            in_specs=[
                pl.BlockSpec((total_rows, tile), lambda n, s: (0, n)),
                pl.BlockSpec((slots, capacity, wide), lambda n, s: (0, 0, 0)),
                pl.BlockSpec((slots * rank, tile), lambda n, s: (0, n)),
            ],
            out_specs=pl.BlockSpec((total_rows, tile), lambda n, s: (0, n)),
            scratch_shapes=[pltpu.VMEM((total_rows, slots * rank), jnp.bfloat16)],
        ),
        compiler_params=pltpu.CompilerParams(vmem_limit_bytes=VMEM_LIMIT),
        cost_estimate=pl.CostEstimate(
            flops=2 * total_rows * slots * rank * columns,
            bytes_accessed=6 * total_rows * columns + 2 * slots * rank * columns,
            transcendentals=0,
        ),
        name="last",
    )(begins, base, shrunk, expand)


def local(tokens, gate_weight, adapter_shrink, adapter_expand, adapter_blocks, adapter_position):
    width = lax.axis_size(AXIS)
    me = lax.axis_index(AXIS)
    shard, depth = tokens.shape
    columns = gate_weight.shape[1]
    rank = adapter_shrink.shape[2]
    total_rows = shard * width
    plane_rows = 4 * shard
    planes = width // 4
    z, y, core = me // 4, (me // 2) % 2, me % 2

    count = adapter_position.shape[0]
    ids = jnp.arange(count, dtype=jnp.int32)
    capacity = MOST * BLOCK
    starts = jnp.sum(jnp.where(ids[None, :] < ids[:, None], adapter_blocks[None, :], 0), axis=1) * BLOCK
    sizes = adapter_blocks * BLOCK
    at_slot = adapter_position[None, :] == ids[:, None]
    start_by_slot = jnp.sum(jnp.where(at_slot, starts[None, :], 0), axis=1)
    size_by_slot = jnp.sum(jnp.where(at_slot, sizes[None, :], 0), axis=1)
    begin_by_slot = jnp.minimum(start_by_slot, total_rows - capacity)

    def at(z_, y_, c_):
        return (z_ * 2 + y_) * 2 + c_

    both = [(a, b, c) for a in range(planes) for b in range(2) for c in range(2)]
    swap_core = [(at(a, b, c), at(a, b, 1 - c)) for a, b, c in both]
    swap_y = [(at(a, b, c), at(a, 1 - b, c)) for a, b, c in both]

    def holds(j, a, c):
        return a >= j if c == 0 else a <= planes - 1 - j

    def along(j):
        up = [(at(a, b, 0), at(a + 1, b, 0)) for a in range(j - 1, planes - 1) for b in range(2)]
        down = [(at(a, b, 1), at(a - 1, b, 1)) for a in range(1, planes - j + 1) for b in range(2)]
        return up + down

    def send(value, pairs):
        return lax.ppermute(value, AXIS, pairs)

    expand_parts = adapter_expand.reshape(rank, width, columns).transpose(1, 0, 2)
    expand = lax.all_to_all(expand_parts, AXIS, split_axis=0, concat_axis=0, tiled=True)

    other_core = send(tokens, swap_core)
    across = send(tokens, swap_y)
    chip = jnp.where(
        core == 0, jnp.concatenate([tokens, other_core]), jnp.concatenate([other_core, tokens])
    )
    across_other = send(across, swap_core)

    shrink_t = jnp.swapaxes(adapter_shrink[0], 0, 1)
    scalars = jnp.stack([z, y, core, 0]).astype(jnp.int32)
    held = plane_matmul(
        functools.partial(fill_own, shard), scalars, [chip, across, across_other], gate_weight, shrink_t, None,
        total_rows, plane_rows,
    )

    order = []
    for a in range(planes):
        found = []
        for j in range(1, planes):
            if a >= j:
                found.append((a - j, j, 0))
            if a <= planes - 1 - j:
                found.append((a + j, j, 1))
        order.append(found)
    table = jnp.asarray(
        [[[p, 2 * (j - 1) + d] for p, j, d in found] for found in order], jnp.int32
    )
    mine = lax.dynamic_index_in_dim(table, z, 0, keepdims=False)

    sources = []
    carried = chip
    for j in range(1, planes):
        swap_yj = [(at(a, b, c), at(a, 1 - b, c)) for a, b, c in both if holds(j, a, c)]
        swap_cj = [(at(a, b, c), at(a, b, 1 - c)) for a, b, c in both if holds(j, a, c)]
        carried = send(carried, along(j))
        carried_across = send(carried, swap_yj)
        sources += [carried, carried_across, send(carried, swap_cj), send(carried_across, swap_cj)]
        pick = mine[j - 1, 1]
        pick = pick - pick % 2 + jnp.where(pick % 2 == core, 0, 1)
        scalars = jnp.stack([mine[j - 1, 0], y, core, pick]).astype(jnp.int32)
        held = plane_matmul(
            functools.partial(fill_far, shard), scalars, list(sources), gate_weight, shrink_t, held,
            total_rows, plane_rows,
        )
    base, shrunk = held

    my_begin, my_start, my_size = begin_by_slot[me], start_by_slot[me], size_by_slot[me]
    rows = my_begin + jnp.arange(capacity, dtype=jnp.int32)
    keep = (rows >= my_start) & (rows < my_start + my_size)
    chosen = lax.dynamic_slice_in_dim(shrunk, my_begin, capacity, 0)
    chosen = jnp.where(keep[:, None], chosen, jnp.zeros_like(chosen))
    chosen = jnp.broadcast_to(chosen[None], (width, capacity, 2 * rank))
    shrunk_all = lax.all_to_all(chosen, AXIS, split_axis=0, concat_axis=0, tiled=True)
    return last(begin_by_slot, base, shrunk_all, expand.reshape(width * rank, columns), rank)


def solution(mesh):
    return jax.shard_map(
        local,
        mesh=mesh,
        in_specs=(
            P(("groups", "tensor"), None),
            P(None, "tensor"),
            P(("groups", "tensor"), None, None),
            P(("groups", "tensor"), None, None),
            P("groups"),
            P("groups"),
        ),
        out_specs=P("groups", "tensor"),
        check_vma=False,
    )
```

```python
import functools

import jax
import jax.numpy as jnp
from jax import lax
from jax.experimental import pallas as pl
from jax.experimental.pallas import tpu as pltpu
from jax.sharding import PartitionSpec as P

BLOCK = 32
MOST = 4
AXIS = "tensor"
VMEM_LIMIT = 56 * 1024 * 1024
ANY = pl.BlockSpec(memory_space=pltpu.HBM)


def tie(values, after):
    count = len(values)

    def body(*refs):
        del refs

    return pl.pallas_call(
        body,
        out_shape=[jax.ShapeDtypeStruct(v.shape, v.dtype) for v in values],
        in_specs=[ANY] * (count + len(after)),
        out_specs=[ANY] * count,
        input_output_aliases={i: i for i in range(count)},
        name="tie",
    )(*values, *after)


def order(values, after):
    return lax.optimization_barrier(tuple(values) + tuple(after))[: len(values)]


def chips_kernel(heights, scalars, *refs):
    count = len(heights)
    pieces = refs[:count]
    weight, shrink_t = refs[count : count + 2]
    out, shrunk, rows, narrow, sem, narrow_sem = refs[-6:]

    def narrow_copies():
        copies = []
        at = 0
        for i, height in enumerate(heights):
            copies.append(
                pltpu.make_async_copy(
                    narrow.at[pl.ds(at, height)],
                    shrunk.at[pl.ds(pl.multiple_of(scalars[i], height), height)],
                    narrow_sem.at[i],
                )
            )
            at += height
        return copies

    @pl.when(pl.program_id(0) == 0)
    def _():
        copies = []
        at = 0
        for i, height in enumerate(heights):
            copies.append(pltpu.make_async_copy(pieces[i], rows.at[pl.ds(at, height)], sem.at[i]))
            copies[-1].start()
            at += height
        for copy in copies:
            copy.wait()
        s = lax.dot_general(
            rows[...], shrink_t[...], (((1,), (1,)), ((), ())), preferred_element_type=jnp.float32
        ).astype(narrow.dtype)
        narrow[...] = jnp.concatenate([s, jnp.zeros_like(s)], axis=1)
        for copy in narrow_copies():
            copy.start()

    out[...] = jnp.dot(rows[...], weight[...], preferred_element_type=jnp.float32)

    @pl.when(pl.program_id(0) == pl.num_programs(0) - 1)
    def _():
        for copy in narrow_copies():
            copy.wait()


def chips_matmul(places, pieces, weight, shrink_t, held, total_rows, after, tile=256):
    depth, columns = weight.shape
    rank = shrink_t.shape[0]
    count = len(pieces)
    heights = [p.shape[0] for p in pieces]
    rows = sum(heights)
    while columns % tile:
        tile //= 2
    extra = ([] if held is None else [held]) + list(after)
    return pl.pallas_call(
        functools.partial(chips_kernel, heights),
        out_shape=[
            jax.ShapeDtypeStruct((rows, columns), jnp.float32),
            jax.ShapeDtypeStruct((total_rows, 2 * rank), jnp.bfloat16),
        ],
        grid_spec=pltpu.PrefetchScalarGridSpec(
            num_scalar_prefetch=1,
            grid=(columns // tile,),
            in_specs=[ANY] * count
            + [
                pl.BlockSpec((depth, tile), lambda n, s: (0, n)),
                pl.BlockSpec((rank, depth), lambda n, s: (0, 0)),
            ]
            + [ANY] * len(extra),
            out_specs=[pl.BlockSpec((rows, tile), lambda n, s: (0, n)), ANY],
            scratch_shapes=[
                pltpu.VMEM((rows, depth), jnp.bfloat16),
                pltpu.VMEM((rows, 2 * rank), jnp.bfloat16),
                pltpu.SemaphoreType.DMA((count,)),
                pltpu.SemaphoreType.DMA((count,)),
            ],
        ),
        input_output_aliases={} if held is None else {3 + count: 1},
        compiler_params=pltpu.CompilerParams(vmem_limit_bytes=VMEM_LIMIT),
        cost_estimate=pl.CostEstimate(
            flops=2 * rows * depth * columns,
            bytes_accessed=2 * depth * columns + 2 * rows * depth + 4 * rows * columns,
            transcendentals=0,
        ),
        name="chips",
    )(jnp.stack(places).astype(jnp.int32), *pieces, weight, shrink_t, *extra)


def spread_kernel(slots, rank, begins, shrunk, spread):
    capacity = shrunk.shape[0] // slots
    spread[...] = jnp.zeros_like(spread)
    for s in range(slots):
        rows = pl.ds(pl.multiple_of(begins[s], BLOCK), capacity)
        spread[rows, s * rank : (s + 1) * rank] = shrunk[s * capacity : (s + 1) * capacity, :rank]


def spread_rows(begins, shrunk, total_rows, rank):
    slots = begins.shape[0]
    return pl.pallas_call(
        functools.partial(spread_kernel, slots, rank),
        out_shape=jax.ShapeDtypeStruct((total_rows, slots * rank), jnp.bfloat16),
        in_specs=[pl.BlockSpec(memory_space=pltpu.SMEM), pl.BlockSpec(memory_space=pltpu.VMEM)],
        out_specs=pl.BlockSpec(memory_space=pltpu.VMEM),
        compiler_params=pltpu.CompilerParams(vmem_limit_bytes=VMEM_LIMIT),
        name="spread",
    )(begins, shrunk)


def last_kernel(parts, scalars, *refs):
    bases = refs[: len(parts)]
    spread, expand, out = refs[len(parts) :]
    i = 0
    for base, heights in zip(bases, parts):
        at = 0
        for height in heights:
            rows = pl.ds(pl.multiple_of(scalars[i], height), height)
            lora = jnp.dot(spread[rows, :], expand[...], preferred_element_type=jnp.float32).astype(jnp.bfloat16)
            out[rows, :] = (base[at : at + height] + lora.astype(jnp.float32)).astype(jnp.bfloat16)
            at += height
            i += 1


def last(places, parts, bases, spread, expand, tile=256):
    total_rows = spread.shape[0]
    inner, columns = expand.shape
    while columns % tile:
        tile //= 2
    return pl.pallas_call(
        functools.partial(last_kernel, parts),
        out_shape=jax.ShapeDtypeStruct((total_rows, columns), jnp.bfloat16),
        grid_spec=pltpu.PrefetchScalarGridSpec(
            num_scalar_prefetch=1,
            grid=(columns // tile,),
            in_specs=[pl.BlockSpec((base.shape[0], tile), lambda n, s: (0, n)) for base in bases]
            + [
                pl.BlockSpec((total_rows, inner), lambda n, s: (0, 0)),
                pl.BlockSpec((inner, tile), lambda n, s: (0, n)),
            ],
            out_specs=pl.BlockSpec((total_rows, tile), lambda n, s: (0, n)),
        ),
        compiler_params=pltpu.CompilerParams(vmem_limit_bytes=VMEM_LIMIT),
        cost_estimate=pl.CostEstimate(
            flops=2 * total_rows * inner * columns,
            bytes_accessed=6 * total_rows * columns + 2 * inner * columns,
            transcendentals=0,
        ),
        name="last",
    )(jnp.stack(places).astype(jnp.int32), *bases, spread, expand)


def local(tokens, gate_weight, adapter_shrink, adapter_expand, adapter_blocks, adapter_position):
    width = lax.axis_size(AXIS)
    me = lax.axis_index(AXIS)
    shard, depth = tokens.shape
    columns = gate_weight.shape[1]
    rank = adapter_shrink.shape[2]
    total_rows = shard * width
    chips = width // 2
    chip_rows = 2 * shard
    chip, core = me // 2, me % 2

    count = adapter_position.shape[0]
    ids = jnp.arange(count, dtype=jnp.int32)
    capacity = MOST * BLOCK
    starts = jnp.sum(jnp.where(ids[None, :] < ids[:, None], adapter_blocks[None, :], 0), axis=1) * BLOCK
    sizes = adapter_blocks * BLOCK
    at_slot = adapter_position[None, :] == ids[:, None]
    start_by_slot = jnp.sum(jnp.where(at_slot, starts[None, :], 0), axis=1)
    size_by_slot = jnp.sum(jnp.where(at_slot, sizes[None, :], 0), axis=1)
    begin_by_slot = jnp.minimum(start_by_slot, total_rows - capacity)

    ring = list(range(0, chips, 2)) + list(range(chips - 1, 0, -2))
    place = [ring.index(a) for a in range(chips)]
    swap_core = [(a * 2 + c, a * 2 + 1 - c) for a in range(chips) for c in range(2)]
    around = [
        (a * 2 + c, ring[(place[a] + 1 - 2 * c) % chips] * 2 + c) for a in range(chips) for c in range(2)
    ]
    behind = jnp.asarray([[ring[(place[a] - j) % chips] for j in range(chips)] for a in range(chips)], jnp.int32)
    behind = lax.dynamic_index_in_dim(behind, chip, 0, keepdims=False)

    def send(value, pairs):
        return lax.ppermute(value, AXIS, pairs)

    shrink_t = jnp.swapaxes(adapter_shrink[0], 0, 1)
    expand_parts = adapter_expand.reshape(rank, width, columns).transpose(1, 0, 2)

    neighbour = send(tokens, swap_core)
    whole = jnp.where(core == 0, jnp.concatenate([tokens, neighbour]), jnp.concatenate([neighbour, tokens]))
    half_way = chips // 2
    carried = send(whole, around)
    pieces, places = [whole], [chip * chip_rows]
    bases, parts, all_places, shrunk = [], [], [], None
    for j in range(1, half_way + 1):
        onward = None
        if j >= 2 and j < half_way:
            carried = order([carried], [shrunk])[0]
        if j + 1 < half_way:
            onward = send(carried, around)
        elif j + 1 == half_way:
            half = jnp.where(core == 0, carried[:shard], carried[shard:])
            onward = send(half, around)
        swapped = send(carried, swap_core)
        mine_from = jnp.where(core == 0, behind[j], behind[chips - j]) * chip_rows
        other_from = jnp.where(core == 0, behind[chips - j], behind[j]) * chip_rows
        if j == half_way:
            mine_from, other_from = mine_from + core * shard, other_from + (1 - core) * shard
            (expand_parts,) = order([expand_parts], [carried, previous])
            expand = lax.all_to_all(expand_parts, AXIS, split_axis=0, concat_axis=0, tiled=True)
        pieces += [carried, swapped]
        places += [mine_from, other_from]
        if j + 1 != half_way:
            base, shrunk = chips_matmul(
                places, pieces, gate_weight, shrink_t, shrunk, total_rows, [] if onward is None else [carried]
            )
            bases.append(base)
            parts.append([p.shape[0] for p in pieces])
            all_places += places
            pieces, places = [], []
        carried, previous = onward, swapped

    my_begin, my_start, my_size = begin_by_slot[me], start_by_slot[me], size_by_slot[me]
    rows = my_begin + jnp.arange(capacity, dtype=jnp.int32)
    keep = (rows >= my_start) & (rows < my_start + my_size)
    chosen = lax.dynamic_slice_in_dim(shrunk, my_begin, capacity, 0)
    chosen = jnp.where(keep[:, None], chosen, jnp.zeros_like(chosen))
    shrunk_all = lax.all_gather(chosen, AXIS, axis=0, tiled=True)
    spread = spread_rows(begin_by_slot.astype(jnp.int32), shrunk_all, total_rows, rank)
    return last(all_places, parts, bases, spread, expand.reshape(width * rank, columns))


def solution(mesh):
    return jax.shard_map(
        local,
        mesh=mesh,
        in_specs=(
            P(("groups", "tensor"), None),
            P(None, "tensor"),
            P(("groups", "tensor"), None, None),
            P(("groups", "tensor"), None, None),
            P("groups"),
            P("groups"),
        ),
        out_specs=P("groups", "tensor"),
        check_vma=False,
    )
```

```python
import functools

import jax
import jax.numpy as jnp
from jax import lax
from jax.experimental import pallas as pl
from jax.experimental.pallas import tpu as pltpu
from jax.sharding import PartitionSpec as P

BLOCK = 32
MOST = 4
AXIS = "tensor"
VMEM_LIMIT = 56 * 1024 * 1024
LANES = 128
ANY = pl.BlockSpec(memory_space=pltpu.HBM)


def order(values, after):
    return lax.optimization_barrier(tuple(values) + tuple(after))[: len(values)]


def parts_kernel(expand, low, high):
    count, tiles, height = low.shape[0], low.shape[1], low.shape[2]
    spare = high.shape[1] - tiles
    for i in range(count):
        for t in range(tiles):
            columns = expand[:, (i * tiles + t) * LANES : (i * tiles + t + 1) * LANES]
            low[i, t] = columns[:height]
            high[i, spare + t] = columns[height:]


def parts_of(expand, height, width, spare):
    rank, columns = expand.shape[0], expand.shape[1] // width
    tiles = columns // LANES
    return pl.pallas_call(
        parts_kernel,
        out_shape=[
            jax.ShapeDtypeStruct((width, tiles, height, LANES), expand.dtype),
            jax.ShapeDtypeStruct((width, tiles + spare, rank - height, LANES), expand.dtype),
        ],
        grid=(width // 4,),
        in_specs=[pl.BlockSpec((rank, 4 * columns), lambda d: (0, d))],
        out_specs=[
            pl.BlockSpec((4, tiles, height, LANES), lambda d: (d, 0, 0, 0)),
            pl.BlockSpec((4, tiles + spare, rank - height, LANES), lambda d: (d, 0, 0, 0)),
        ],
        compiler_params=pltpu.CompilerParams(vmem_limit_bytes=VMEM_LIMIT),
        cost_estimate=pl.CostEstimate(flops=0, bytes_accessed=4 * rank * columns * width, transcendentals=0),
        name="parts",
    )(expand)


def shrink_kernel(count, scalars, *refs):
    pieces = refs[:count]
    shrink_t, _, out, rows, packed, sem, out_sem = refs[count:]
    shard = pieces[0].shape[0]
    begin, start, size = scalars[count], scalars[count + 1], scalars[count + 2]

    for b in range(MOST):
        first = begin + b * BLOCK
        inside = lax.rem(first, shard)

        for i in range(count):

            @pl.when(scalars[i] == first - inside)
            def _():
                pltpu.make_async_copy(
                    pieces[i].at[pl.ds(pl.multiple_of(inside, BLOCK), BLOCK)],
                    rows.at[pl.ds(b * BLOCK, BLOCK)],
                    sem.at[b],
                ).start()

    for b in range(MOST):
        pltpu.make_async_copy(
            pieces[0].at[pl.ds(0, BLOCK)], rows.at[pl.ds(b * BLOCK, BLOCK)], sem.at[b]
        ).wait()

    s = lax.dot_general(rows[...], shrink_t[...], (((1,), (1,)), ((), ())), preferred_element_type=jnp.float32)
    row = begin + lax.broadcasted_iota(jnp.int32, s.shape, 0)
    s = jnp.where((row >= start) & (row < start + size), s, 0.0).astype(out.dtype)
    spare, height = packed.shape[0], packed.shape[1]
    half = MOST * BLOCK // 2
    both = jnp.concatenate([s[:half], s[half:]], axis=1)
    for i in range(spare):
        some = both[i * height : (i + 1) * height]
        packed[i, : some.shape[0]] = some
    copies = [
        pltpu.make_async_copy(packed, out.at[d, pl.ds(0, spare)], out_sem.at[d]) for d in range(out.shape[0])
    ]
    for copy in copies:
        copy.start()
    for copy in copies:
        copy.wait()


def shrink_rows(scalars, pieces, shrink_t, operand, spare):
    rank, depth = shrink_t.shape
    count = len(pieces)
    return pl.pallas_call(
        functools.partial(shrink_kernel, count),
        out_shape=jax.ShapeDtypeStruct(operand.shape, operand.dtype),
        in_specs=[pl.BlockSpec(memory_space=pltpu.SMEM)]
        + [ANY] * count
        + [pl.BlockSpec(memory_space=pltpu.VMEM), ANY],
        out_specs=ANY,
        scratch_shapes=[
            pltpu.VMEM((MOST * BLOCK, depth), jnp.bfloat16),
            pltpu.VMEM((spare,) + operand.shape[2:], jnp.bfloat16),
            pltpu.SemaphoreType.DMA((MOST,)),
            pltpu.SemaphoreType.DMA((operand.shape[0],)),
        ],
        input_output_aliases={2 + count: 0},
        compiler_params=pltpu.CompilerParams(vmem_limit_bytes=VMEM_LIMIT),
        cost_estimate=pl.CostEstimate(
            flops=2 * MOST * BLOCK * depth * rank, bytes_accessed=2 * MOST * BLOCK * depth, transcendentals=0
        ),
        name="shrink",
    )(scalars, *pieces, shrink_t, operand)


def base_kernel(count, scalars, *refs):
    pieces = refs[:count]
    weight, (out, rows, sem) = refs[count], refs[-3:]
    shard = pieces[0].shape[0]
    total = count * shard

    def copy(i):
        return pltpu.make_async_copy(pieces[i], rows.at[pl.ds(i * shard, shard)], sem.at[i])

    def product(first, last):
        found = jnp.dot(
            rows[first * shard : last * shard], weight[...], preferred_element_type=jnp.float32
        )
        for i in range(first, last):
            out[pl.ds(pl.multiple_of(scalars[i], shard), shard), :] = found[(i - first) * shard : (i - first + 1) * shard]

    @pl.when(pl.program_id(0) == 0)
    def _():
        for i in range(count):
            copy(i).start()
        for part in range(2):
            some = range(part * count // 2, (part + 1) * count // 2)
            for i in some:
                copy(i).wait()
            product(some[0], some[-1] + 1)

    @pl.when(pl.program_id(0) > 0)
    def _():
        product(0, count)


def base_matmul(places, pieces, weight, held, first, steps, tile):
    depth, columns = weight.shape
    count = len(pieces)
    rows = count * pieces[0].shape[0]
    extra = [] if held is None else [held]
    return pl.pallas_call(
        functools.partial(base_kernel, count),
        out_shape=jax.ShapeDtypeStruct((rows, columns), jnp.float32),
        grid_spec=pltpu.PrefetchScalarGridSpec(
            num_scalar_prefetch=1,
            grid=(steps,),
            in_specs=[ANY] * count + [pl.BlockSpec((depth, tile), lambda n, s: (0, first + n))] + [ANY] * len(extra),
            out_specs=pl.BlockSpec((rows, tile), lambda n, s: (0, first + n)),
            scratch_shapes=[pltpu.VMEM((rows, depth), jnp.bfloat16), pltpu.SemaphoreType.DMA((count,))],
        ),
        compiler_params=pltpu.CompilerParams(vmem_limit_bytes=VMEM_LIMIT),
        cost_estimate=pl.CostEstimate(
            flops=2 * rows * depth * tile * steps,
            bytes_accessed=2 * depth * tile * steps + 2 * rows * depth + 4 * rows * tile * steps,
            transcendentals=0,
        ),
        input_output_aliases={} if held is None else {count + 2: 0},
        name="base",
    )(places, *pieces, weight, *extra)


def last_kernel(spare, begins, base, shrunk, low, high, out, spread):
    width, tiles, height = low.shape[0], low.shape[1], low.shape[2]
    inner, others = width * height, high.shape[2]

    @pl.when(pl.program_id(0) == 0)
    def _():
        spread[...] = jnp.zeros_like(spread)
        half = LANES // 2
        for s in range(width):
            both = jnp.concatenate([shrunk[s, i] for i in range(spare)], axis=0)[:half]
            for h in range(2):
                rows = pl.ds(pl.multiple_of(begins[s] + h * half, BLOCK), half)
                mine = both[:, h * half : (h + 1) * half]
                spread[rows, s * height : (s + 1) * height] = mine[:, :height]
                spread[rows, inner + s * others : inner + (s + 1) * others] = mine[:, height:]

    expand = jnp.concatenate(
        [
            jnp.concatenate([part[:, t].reshape(width * part.shape[2], LANES) for t in range(tiles)], axis=1)
            for part in (low, high)
        ],
        axis=0,
    )
    lora = jnp.dot(spread[...], expand, preferred_element_type=jnp.float32).astype(jnp.bfloat16)
    out[...] = (base[...] + lora.astype(jnp.float32)).astype(jnp.bfloat16)


def last(begins, base, low, high, spare):
    total_rows, columns = base.shape
    width, all_tiles, height, _ = low.shape
    others = high.shape[2]
    tiles = 2 if all_tiles % 2 == 0 and spare % 2 == 0 else 1
    tile = tiles * LANES
    return pl.pallas_call(
        functools.partial(last_kernel, spare),
        out_shape=jax.ShapeDtypeStruct((total_rows, columns), jnp.bfloat16),
        grid_spec=pltpu.PrefetchScalarGridSpec(
            num_scalar_prefetch=1,
            grid=(columns // tile,),
            in_specs=[
                pl.BlockSpec((total_rows, tile), lambda n, s: (0, n)),
                pl.BlockSpec((width, spare, others, LANES), lambda n, s: (0, 0, 0, 0)),
                pl.BlockSpec((width, tiles, height, LANES), lambda n, s: (0, n, 0, 0)),
                pl.BlockSpec((width, tiles, others, LANES), lambda n, s: (0, n + spare // tiles, 0, 0)),
            ],
            out_specs=pl.BlockSpec((total_rows, tile), lambda n, s: (0, n)),
            scratch_shapes=[pltpu.VMEM((total_rows, width * (height + others)), jnp.bfloat16)],
        ),
        compiler_params=pltpu.CompilerParams(vmem_limit_bytes=VMEM_LIMIT),
        cost_estimate=pl.CostEstimate(
            flops=2 * total_rows * width * (height + others) * columns,
            bytes_accessed=6 * total_rows * columns + 2 * width * (height + others) * columns,
            transcendentals=0,
        ),
        name="last",
    )(begins, base, high, low, high)


def local(tokens, gate_weight, adapter_shrink, adapter_expand, adapter_blocks, adapter_position):
    width = lax.axis_size(AXIS)
    me = lax.axis_index(AXIS)
    shard, depth = tokens.shape
    columns = gate_weight.shape[1]
    rank = adapter_shrink.shape[2]
    total_rows = shard * width
    chips = width // 2
    chip_rows = 2 * shard
    chip, core = me // 2, me % 2

    count = adapter_position.shape[0]
    ids = jnp.arange(count, dtype=jnp.int32)
    capacity = MOST * BLOCK
    starts = jnp.sum(jnp.where(ids[None, :] < ids[:, None], adapter_blocks[None, :], 0), axis=1) * BLOCK
    sizes = adapter_blocks * BLOCK
    at_slot = adapter_position[None, :] == ids[:, None]
    start_by_slot = jnp.sum(jnp.where(at_slot, starts[None, :], 0), axis=1)
    size_by_slot = jnp.sum(jnp.where(at_slot, sizes[None, :], 0), axis=1)
    begin_by_slot = jnp.minimum(start_by_slot, total_rows - capacity)

    ring = list(range(0, chips, 2)) + list(range(chips - 1, 0, -2))
    place = [ring.index(a) for a in range(chips)]
    swap_core = [(a * 2 + c, a * 2 + 1 - c) for a in range(chips) for c in range(2)]
    around = [
        (a * 2 + c, ring[(place[a] + 1 - 2 * c) % chips] * 2 + c) for a in range(chips) for c in range(2)
    ]
    behind = jnp.asarray([[ring[(place[a] - j) % chips] for j in range(chips)] for a in range(chips)], jnp.int32)
    behind = lax.dynamic_index_in_dim(behind, chip, 0, keepdims=False)

    def send(value, pairs):
        return lax.ppermute(value, AXIS, pairs)

    shrink_t = jnp.swapaxes(adapter_shrink[0], 0, 1)
    height = rank // 2
    spare = -(-(MOST * BLOCK // 2) // (rank - height))

    low, high = parts_of(adapter_expand[0], height, width, spare)
    half_way = chips // 2
    first = send(tokens, around)
    neighbour = send(tokens, swap_core)
    second = send(neighbour, around)
    pieces = [tokens, neighbour]
    places = [me * shard, (chip * 2 + 1 - core) * shard]
    swapped = [neighbour]
    for j in range(1, half_way + 1):
        mine_from = jnp.where(core == 0, behind[j], behind[chips - j]) * 2
        other_from = jnp.where(core == 0, behind[chips - j], behind[j]) * 2
        if j < half_way:
            first, second = order([first, second], swapped + [low, high])
            next_first = send(first, around)
            next_second = send(second, around) if j + 1 < half_way else None
            swapped = [send(first, swap_core), send(second, swap_core)]
            pieces += [first, second] + swapped
            places += [
                (mine_from + core) * shard,
                (mine_from + 1 - core) * shard,
                (other_from + 1 - core) * shard,
                (other_from + core) * shard,
            ]
            first, second = next_first, next_second
        else:
            low = order([low], [first] + swapped)[0]
            swapped.append(send(first, swap_core))
            low = lax.all_to_all(low, AXIS, split_axis=0, concat_axis=0, tiled=True)
            pieces += [first, swapped[-1]]
            places += [(mine_from + core) * shard, (other_from + 1 - core) * shard]
    places = jnp.stack(places).astype(jnp.int32)

    mine = jnp.stack([begin_by_slot[me], start_by_slot[me], size_by_slot[me]])
    scalars = jnp.concatenate([places, mine]).astype(jnp.int32)
    high = shrink_rows(scalars, pieces, shrink_t, high, spare)
    tile = 256
    while columns % tile or total_rows * tile > 1024 * 256:
        tile //= 2
    steps = columns // tile
    early = max(steps // 7, 1)
    places = order([places], [high])[0]
    base = base_matmul(places, pieces, gate_weight, None, 0, early, tile)
    high, base, places = order([high, base, places], [low])
    high = lax.all_to_all(high, AXIS, split_axis=0, concat_axis=0, tiled=True)
    base = base_matmul(places, pieces, gate_weight, base, early, steps - early, tile)
    return last(begin_by_slot.astype(jnp.int32), base, low, high, spare)


def solution(mesh):
    return jax.shard_map(
        local,
        mesh=mesh,
        in_specs=(
            P(("groups", "tensor"), None),
            P(None, "tensor"),
            P(("groups", "tensor"), None, None),
            P(("groups", "tensor"), None, None),
            P("groups"),
            P("groups"),
        ),
        out_specs=P("groups", "tensor"),
        check_vma=False,
    )
```

```python
import functools

import jax
import jax.numpy as jnp
from jax import lax
from jax.experimental import pallas as pl
from jax.experimental.pallas import tpu as pltpu
from jax.sharding import PartitionSpec as P

BLOCK = 32
MOST = 4
AXIS = "tensor"
VMEM_LIMIT = 56 * 1024 * 1024
LANES = 128
ANY = pl.BlockSpec(memory_space=pltpu.HBM)


def order(values, after):
    return lax.optimization_barrier(tuple(values) + tuple(after))[: len(values)]


def parts_kernel(expand, low, high):
    count, tiles, height = low.shape[0], low.shape[1], low.shape[2]
    spare = high.shape[1] - tiles
    for i in range(count):
        for t in range(tiles):
            columns = expand[:, (i * tiles + t) * LANES : (i * tiles + t + 1) * LANES]
            low[i, t] = columns[:height]
            high[i, spare + t] = columns[height:]


def parts_of(expand, height, width, spare):
    rank, columns = expand.shape[0], expand.shape[1] // width
    tiles = columns // LANES
    return pl.pallas_call(
        parts_kernel,
        out_shape=[
            jax.ShapeDtypeStruct((width, tiles, height, LANES), expand.dtype),
            jax.ShapeDtypeStruct((width, tiles + spare, rank - height, LANES), expand.dtype),
        ],
        grid=(width // 4,),
        in_specs=[pl.BlockSpec((rank, 4 * columns), lambda d: (0, d))],
        out_specs=[
            pl.BlockSpec((4, tiles, height, LANES), lambda d: (d, 0, 0, 0)),
            pl.BlockSpec((4, tiles + spare, rank - height, LANES), lambda d: (d, 0, 0, 0)),
        ],
        compiler_params=pltpu.CompilerParams(vmem_limit_bytes=VMEM_LIMIT),
        cost_estimate=pl.CostEstimate(flops=0, bytes_accessed=4 * rank * columns * width, transcendentals=0),
        name="parts",
    )(expand)


def shrink_kernel(count, scalars, *refs):
    pieces = refs[:count]
    shrink_t, _, out, rows, packed, sem, out_sem = refs[count:]
    shard = pieces[0].shape[0]
    begin, start, size = scalars[count], scalars[count + 1], scalars[count + 2]

    for b in range(MOST):
        first = begin + b * BLOCK
        inside = lax.rem(first, shard)

        for i in range(count):

            @pl.when(scalars[i] == first - inside)
            def _():
                pltpu.make_async_copy(
                    pieces[i].at[pl.ds(pl.multiple_of(inside, BLOCK), BLOCK)],
                    rows.at[pl.ds(b * BLOCK, BLOCK)],
                    sem.at[b],
                ).start()

    for b in range(MOST):
        pltpu.make_async_copy(
            pieces[0].at[pl.ds(0, BLOCK)], rows.at[pl.ds(b * BLOCK, BLOCK)], sem.at[b]
        ).wait()

    s = lax.dot_general(rows[...], shrink_t[...], (((1,), (1,)), ((), ())), preferred_element_type=jnp.float32)
    row = begin + lax.broadcasted_iota(jnp.int32, s.shape, 0)
    s = jnp.where((row >= start) & (row < start + size), s, 0.0).astype(out.dtype)
    spare, height = packed.shape[0], packed.shape[1]
    half = MOST * BLOCK // 2
    both = jnp.concatenate([s[:half], s[half:]], axis=1)
    for i in range(spare):
        some = both[i * height : (i + 1) * height]
        packed[i, : some.shape[0]] = some
    copies = [
        pltpu.make_async_copy(packed, out.at[d, pl.ds(0, spare)], out_sem.at[d]) for d in range(out.shape[0])
    ]
    for copy in copies:
        copy.start()
    for copy in copies:
        copy.wait()


def shrink_rows(scalars, pieces, shrink_t, operand, spare):
    rank, depth = shrink_t.shape
    count = len(pieces)
    return pl.pallas_call(
        functools.partial(shrink_kernel, count),
        out_shape=jax.ShapeDtypeStruct(operand.shape, operand.dtype),
        in_specs=[pl.BlockSpec(memory_space=pltpu.SMEM)]
        + [ANY] * count
        + [pl.BlockSpec(memory_space=pltpu.VMEM), ANY],
        out_specs=ANY,
        scratch_shapes=[
            pltpu.VMEM((MOST * BLOCK, depth), jnp.bfloat16),
            pltpu.VMEM((spare,) + operand.shape[2:], jnp.bfloat16),
            pltpu.SemaphoreType.DMA((MOST,)),
            pltpu.SemaphoreType.DMA((operand.shape[0],)),
        ],
        input_output_aliases={2 + count: 0},
        compiler_params=pltpu.CompilerParams(vmem_limit_bytes=VMEM_LIMIT),
        cost_estimate=pl.CostEstimate(
            flops=2 * MOST * BLOCK * depth * rank, bytes_accessed=2 * MOST * BLOCK * depth, transcendentals=0
        ),
        name="shrink",
    )(scalars, *pieces, shrink_t, operand)


def base_kernel(count, *refs):
    pieces = refs[:count]
    weight, out, rows, sem = refs[count:]
    shard = pieces[0].shape[0]

    @pl.when(pl.program_id(0) == 0)
    def _():
        copies = [
            pltpu.make_async_copy(pieces[i], rows.at[pl.ds(i * shard, shard)], sem.at[i]) for i in range(count)
        ]
        for copy in copies:
            copy.start()
        for copy in copies:
            copy.wait()

    out[...] = jnp.dot(rows[...], weight[...], preferred_element_type=jnp.float32)


def base_matmul(pieces, weight, share=1, tile=256):
    depth, columns = weight.shape
    count = len(pieces)
    rows = count * pieces[0].shape[0]
    while columns % tile:
        tile //= 2
    return pl.pallas_call(
        functools.partial(base_kernel, count),
        out_shape=jax.ShapeDtypeStruct((rows, columns), jnp.float32),
        grid=(columns // tile,),
        in_specs=[ANY] * count + [pl.BlockSpec((depth, tile), lambda n: (0, n))],
        out_specs=pl.BlockSpec((rows, tile), lambda n: (0, n)),
        scratch_shapes=[pltpu.VMEM((rows, depth), jnp.bfloat16), pltpu.SemaphoreType.DMA((count,))],
        compiler_params=pltpu.CompilerParams(vmem_limit_bytes=VMEM_LIMIT),
        cost_estimate=pl.CostEstimate(
            flops=2 * rows * depth * columns * share,
            bytes_accessed=2 * depth * columns + 2 * rows * depth + 4 * rows * columns,
            transcendentals=0,
        ),
        name="base",
    )(*pieces, weight)


def last_kernel(spare, shard, scalars, *refs):
    bases = refs[:2]
    shrunk, low, high, out, spread, lora = refs[2:]
    width, tiles, height = low.shape[0], low.shape[1], low.shape[2]
    inner, others = width * height, high.shape[2]

    @pl.when(pl.program_id(0) == 0)
    def _():
        spread[...] = jnp.zeros_like(spread)
        half = LANES // 2
        for s in range(width):
            both = jnp.concatenate([shrunk[s, i] for i in range(spare)], axis=0)[:half]
            for h in range(2):
                rows = pl.ds(pl.multiple_of(scalars[s] + h * half, BLOCK), half)
                mine = both[:, h * half : (h + 1) * half]
                spread[rows, s * height : (s + 1) * height] = mine[:, :height]
                spread[rows, inner + s * others : inner + (s + 1) * others] = mine[:, height:]

    expand = jnp.concatenate(
        [
            jnp.concatenate([part[:, t].reshape(width * part.shape[2], LANES) for t in range(tiles)], axis=1)
            for part in (low, high)
        ],
        axis=0,
    )
    lora[...] = jnp.dot(spread[...], expand, preferred_element_type=jnp.float32)
    i = width
    for base in bases:
        for at in range(0, base.shape[0], shard):
            rows = pl.ds(pl.multiple_of(scalars[i], shard), shard)
            rounded = lora[rows, :].astype(jnp.bfloat16).astype(jnp.float32)
            out[rows, :] = (base[at : at + shard] + rounded).astype(jnp.bfloat16)
            i += 1


def last(scalars, bases, low, high, spare, shard):
    total_rows, columns = sum(b.shape[0] for b in bases), bases[0].shape[1]
    width, all_tiles, height, _ = low.shape
    others = high.shape[2]
    tiles = 2 if all_tiles % 2 == 0 and spare % 2 == 0 else 1
    tile = tiles * LANES
    return pl.pallas_call(
        functools.partial(last_kernel, spare, shard),
        out_shape=jax.ShapeDtypeStruct((total_rows, columns), jnp.bfloat16),
        grid_spec=pltpu.PrefetchScalarGridSpec(
            num_scalar_prefetch=1,
            grid=(columns // tile,),
            in_specs=[
                pl.BlockSpec((bases[0].shape[0], tile), lambda n, s: (0, n)),
                pl.BlockSpec((bases[1].shape[0], tile), lambda n, s: (0, n)),
                pl.BlockSpec((width, spare, others, LANES), lambda n, s: (0, 0, 0, 0)),
                pl.BlockSpec((width, tiles, height, LANES), lambda n, s: (0, n, 0, 0)),
                pl.BlockSpec((width, tiles, others, LANES), lambda n, s: (0, n + spare // tiles, 0, 0)),
            ],
            out_specs=pl.BlockSpec((total_rows, tile), lambda n, s: (0, n)),
            scratch_shapes=[
                pltpu.VMEM((total_rows, width * (height + others)), jnp.bfloat16),
                pltpu.VMEM((total_rows, tile), jnp.float32),
            ],
        ),
        compiler_params=pltpu.CompilerParams(vmem_limit_bytes=VMEM_LIMIT),
        cost_estimate=pl.CostEstimate(
            flops=2 * total_rows * width * (height + others) * columns,
            bytes_accessed=6 * total_rows * columns + 2 * width * (height + others) * columns,
            transcendentals=0,
        ),
        name="last",
    )(scalars, *bases, high, low, high)


def local(tokens, gate_weight, adapter_shrink, adapter_expand, adapter_blocks, adapter_position):
    width = lax.axis_size(AXIS)
    me = lax.axis_index(AXIS)
    shard, depth = tokens.shape
    columns = gate_weight.shape[1]
    rank = adapter_shrink.shape[2]
    total_rows = shard * width
    planes = width // 4
    z, y, core = me // 4, (me // 2) % 2, me % 2

    count = adapter_position.shape[0]
    ids = jnp.arange(count, dtype=jnp.int32)
    capacity = MOST * BLOCK
    starts = jnp.sum(jnp.where(ids[None, :] < ids[:, None], adapter_blocks[None, :], 0), axis=1) * BLOCK
    sizes = adapter_blocks * BLOCK
    at_slot = adapter_position[None, :] == ids[:, None]
    start_by_slot = jnp.sum(jnp.where(at_slot, starts[None, :], 0), axis=1)
    size_by_slot = jnp.sum(jnp.where(at_slot, sizes[None, :], 0), axis=1)
    begin_by_slot = jnp.minimum(start_by_slot, total_rows - capacity)

    def at(z_, y_, core_):
        return (z_ * 2 + y_) * 2 + core_

    both = [(a, b, c) for a in range(planes) for b in range(2) for c in range(2)]
    swap_core = [(at(a, b, c), at(a, b, 1 - c)) for a, b, c in both]
    swap_y = [(at(a, b, c), at(a, 1 - b, c)) for a, b, c in both]
    ring = [0] + list(range(1, planes, 2)) + list(range((planes - 1) // 2 * 2, 0, -2))
    place = [ring.index(a) for a in range(planes)]
    around = [(at(a, b, c), at(ring[(place[a] + 1) % planes], b, c)) for a, b, c in both]
    origin = jnp.asarray([[ring[(place[a] - j) % planes] for j in range(planes)] for a in range(planes)], jnp.int32)
    origin = lax.dynamic_index_in_dim(origin, z, 0, keepdims=False)

    def send(value, pairs):
        return lax.ppermute(value, AXIS, pairs)

    shrink_t = jnp.swapaxes(adapter_shrink[0], 0, 1)
    height = 3 * rank // 4
    spare = -(-(MOST * BLOCK // 2) // (rank - height))

    low, high = parts_of(adapter_expand[0], height, width, spare)
    coming, across = send(tokens, around), send(tokens, swap_y)
    mine, mine_other = tokens, send(tokens, swap_core)
    before = [low, high]
    pieces, places, bases = [], [], []
    some = 2 * planes
    for j in range(planes):
        last_one = j == planes - 1
        if not last_one:
            coming, across = order([coming, across], before)
            onward = send(coming, around) if j + 2 < planes else None
            onward_across = send(coming, swap_y)
            coming_other = send(coming, swap_core)
        else:
            across = order([across], bases)[0]
        across_other = send(across, swap_core)
        before = [across_other] if last_one else [coming_other, across_other]
        if j + 2 == planes:
            low = order([low], [coming])[0]
            low = lax.all_to_all(low, AXIS, split_axis=0, concat_axis=0, tiled=True)
            arrays = pieces[:some]
            arrays = order(arrays, [coming])
            bases.append(base_matmul(arrays, gate_weight, 4))
        pieces += [mine, across, mine_other, across_other]
        for core_ in (core, 1 - core):
            for y_ in (y, 1 - y):
                places.append(((origin[j] * 2 + y_) * 2 + core_) * shard)
        if not last_one:
            mine, mine_other, coming, across = coming, coming_other, onward, onward_across
    places = jnp.stack(places).astype(jnp.int32)

    mine = jnp.stack([begin_by_slot[me], start_by_slot[me], size_by_slot[me]])
    scalars = jnp.concatenate([places, mine]).astype(jnp.int32)
    high = shrink_rows(scalars, pieces, shrink_t, high, spare)
    high = order([high], [low])[0]
    arrays = order(pieces[some:], [high])
    high = lax.all_to_all(high, AXIS, split_axis=0, concat_axis=0, tiled=True)
    bases.append(base_matmul(arrays, gate_weight))
    scalars = jnp.concatenate([begin_by_slot.astype(jnp.int32), places])
    return last(scalars, bases, low, high, spare, shard)


def solution(mesh):
    return jax.shard_map(
        local,
        mesh=mesh,
        in_specs=(
            P(("groups", "tensor"), None),
            P(None, "tensor"),
            P(("groups", "tensor"), None, None),
            P(("groups", "tensor"), None, None),
            P("groups"),
            P("groups"),
        ),
        out_specs=P("groups", "tensor"),
        check_vma=False,
    )
```

```python
import functools

import jax
import jax.numpy as jnp
from jax import lax
from jax.experimental import pallas as pl
from jax.experimental.pallas import tpu as pltpu
from jax.sharding import PartitionSpec as P

BLOCK = 32
MOST = 4
AXIS = "tensor"
VMEM_LIMIT = 56 * 1024 * 1024
LANES = 128
ANY = pl.BlockSpec(memory_space=pltpu.HBM)


def order(values, after):
    return lax.optimization_barrier(tuple(values) + tuple(after))[: len(values)]


def parts_kernel(expand, low, high):
    count, tiles, height = low.shape[0], low.shape[1], low.shape[2]
    spare = high.shape[1] - tiles
    for i in range(count):
        for t in range(tiles):
            columns = expand[:, (i * tiles + t) * LANES : (i * tiles + t + 1) * LANES]
            low[i, t] = columns[:height]
            high[i, spare + t] = columns[height:]


def parts_of(expand, height, width, spare):
    rank, columns = expand.shape[0], expand.shape[1] // width
    tiles = columns // LANES
    return pl.pallas_call(
        parts_kernel,
        out_shape=[
            jax.ShapeDtypeStruct((width, tiles, height, LANES), expand.dtype),
            jax.ShapeDtypeStruct((width, tiles + spare, rank - height, LANES), expand.dtype),
        ],
        grid=(width // 4,),
        in_specs=[pl.BlockSpec((rank, 4 * columns), lambda d: (0, d))],
        out_specs=[
            pl.BlockSpec((4, tiles, height, LANES), lambda d: (d, 0, 0, 0)),
            pl.BlockSpec((4, tiles + spare, rank - height, LANES), lambda d: (d, 0, 0, 0)),
        ],
        compiler_params=pltpu.CompilerParams(vmem_limit_bytes=VMEM_LIMIT),
        cost_estimate=pl.CostEstimate(flops=0, bytes_accessed=4 * rank * columns * width, transcendentals=0),
        name="parts",
    )(expand)


def shrink_kernel(count, scalars, *refs):
    pieces = refs[:count]
    shrink_t, _, out, rows, packed, sem, out_sem = refs[count:]
    shard = pieces[0].shape[0]
    begin, start, size = scalars[count], scalars[count + 1], scalars[count + 2]

    for b in range(MOST):
        first = begin + b * BLOCK
        inside = lax.rem(first, shard)

        for i in range(count):

            @pl.when(scalars[i] == first - inside)
            def _():
                pltpu.make_async_copy(
                    pieces[i].at[pl.ds(pl.multiple_of(inside, BLOCK), BLOCK)],
                    rows.at[pl.ds(b * BLOCK, BLOCK)],
                    sem.at[b],
                ).start()

    for b in range(MOST):
        pltpu.make_async_copy(
            pieces[0].at[pl.ds(0, BLOCK)], rows.at[pl.ds(b * BLOCK, BLOCK)], sem.at[b]
        ).wait()

    s = lax.dot_general(rows[...], shrink_t[...], (((1,), (1,)), ((), ())), preferred_element_type=jnp.float32)
    row = begin + lax.broadcasted_iota(jnp.int32, s.shape, 0)
    s = jnp.where((row >= start) & (row < start + size), s, 0.0).astype(out.dtype)
    spare, height = packed.shape[0], packed.shape[1]
    half = MOST * BLOCK // 2
    both = jnp.concatenate([s[:half], s[half:]], axis=1)
    for i in range(spare):
        some = both[i * height : (i + 1) * height]
        packed[i, : some.shape[0]] = some
    copies = [
        pltpu.make_async_copy(packed, out.at[d, pl.ds(0, spare)], out_sem.at[d]) for d in range(out.shape[0])
    ]
    for copy in copies:
        copy.start()
    for copy in copies:
        copy.wait()


def shrink_rows(scalars, pieces, shrink_t, operand, spare):
    rank, depth = shrink_t.shape
    count = len(pieces)
    return pl.pallas_call(
        functools.partial(shrink_kernel, count),
        out_shape=jax.ShapeDtypeStruct(operand.shape, operand.dtype),
        in_specs=[pl.BlockSpec(memory_space=pltpu.SMEM)]
        + [ANY] * count
        + [pl.BlockSpec(memory_space=pltpu.VMEM), ANY],
        out_specs=ANY,
        scratch_shapes=[
            pltpu.VMEM((MOST * BLOCK, depth), jnp.bfloat16),
            pltpu.VMEM((spare,) + operand.shape[2:], jnp.bfloat16),
            pltpu.SemaphoreType.DMA((MOST,)),
            pltpu.SemaphoreType.DMA((operand.shape[0],)),
        ],
        input_output_aliases={2 + count: 0},
        compiler_params=pltpu.CompilerParams(vmem_limit_bytes=VMEM_LIMIT),
        cost_estimate=pl.CostEstimate(
            flops=2 * MOST * BLOCK * depth * rank, bytes_accessed=2 * MOST * BLOCK * depth, transcendentals=0
        ),
        name="shrink",
    )(scalars, *pieces, shrink_t, operand)


def base_kernel(count, *refs):
    pieces = refs[:count]
    weight, out, rows, sem = refs[count:]
    shard = pieces[0].shape[0]

    @pl.when(pl.program_id(0) == 0)
    def _():
        copies = [
            pltpu.make_async_copy(pieces[i], rows.at[pl.ds(i * shard, shard)], sem.at[i]) for i in range(count)
        ]
        for copy in copies:
            copy.start()
        for copy in copies:
            copy.wait()

    out[...] = jnp.dot(rows[...], weight[...], preferred_element_type=jnp.float32)


def base_matmul(pieces, weight, share=1, tile=256):
    depth, columns = weight.shape
    count = len(pieces)
    rows = count * pieces[0].shape[0]
    while columns % tile:
        tile //= 2
    return pl.pallas_call(
        functools.partial(base_kernel, count),
        out_shape=jax.ShapeDtypeStruct((rows, columns), jnp.float32),
        grid=(columns // tile,),
        in_specs=[ANY] * count + [pl.BlockSpec((depth, tile), lambda n: (0, n))],
        out_specs=pl.BlockSpec((rows, tile), lambda n: (0, n)),
        scratch_shapes=[pltpu.VMEM((rows, depth), jnp.bfloat16), pltpu.SemaphoreType.DMA((count,))],
        compiler_params=pltpu.CompilerParams(vmem_limit_bytes=VMEM_LIMIT),
        cost_estimate=pl.CostEstimate(
            flops=2 * rows * depth * columns * share,
            bytes_accessed=2 * depth * columns + 2 * rows * depth + 4 * rows * columns,
            transcendentals=0,
        ),
        name="base",
    )(*pieces, weight)


def last_kernel(spare, shard, scalars, *refs):
    bases = refs[:2]
    shrunk, low, high, out, spread, lora = refs[2:]
    width, tiles, height = low.shape[0], low.shape[1], low.shape[2]
    rank = height + high.shape[2]

    @pl.when(pl.program_id(0) == 0)
    def _():
        spread[...] = jnp.zeros_like(spread)
        half = rank
        for s in range(width):
            both = jnp.concatenate([shrunk[s, i] for i in range(spare)], axis=0)[:half]
            for h in range(2):
                rows = pl.ds(pl.multiple_of(scalars[s] + h * half, BLOCK), half)
                spread[rows, s * rank : (s + 1) * rank] = both[:, h * half : (h + 1) * half]

    expand = jnp.concatenate(
        [
            jnp.concatenate([low[:, t], high[:, t]], axis=1).reshape(width * rank, LANES)
            for t in range(tiles)
        ],
        axis=1,
    )
    lora[...] = jnp.dot(spread[...], expand, preferred_element_type=jnp.float32)
    i = width
    for base in bases:
        for at in range(0, base.shape[0], shard):
            rows = pl.ds(pl.multiple_of(scalars[i], shard), shard)
            rounded = lora[rows, :].astype(jnp.bfloat16).astype(jnp.float32)
            out[rows, :] = (base[at : at + shard] + rounded).astype(jnp.bfloat16)
            i += 1


def last(scalars, bases, low, high, spare, shard):
    total_rows, columns = sum(b.shape[0] for b in bases), bases[0].shape[1]
    width, all_tiles, height, _ = low.shape
    others = high.shape[2]
    tiles = 2 if all_tiles % 2 == 0 and spare % 2 == 0 else 1
    tile = tiles * LANES
    return pl.pallas_call(
        functools.partial(last_kernel, spare, shard),
        out_shape=jax.ShapeDtypeStruct((total_rows, columns), jnp.bfloat16),
        grid_spec=pltpu.PrefetchScalarGridSpec(
            num_scalar_prefetch=1,
            grid=(columns // tile,),
            in_specs=[
                pl.BlockSpec((bases[0].shape[0], tile), lambda n, s: (0, n)),
                pl.BlockSpec((bases[1].shape[0], tile), lambda n, s: (0, n)),
                pl.BlockSpec((width, spare, others, LANES), lambda n, s: (0, 0, 0, 0)),
                pl.BlockSpec((width, tiles, height, LANES), lambda n, s: (0, n, 0, 0)),
                pl.BlockSpec((width, tiles, others, LANES), lambda n, s: (0, n + spare // tiles, 0, 0)),
            ],
            out_specs=pl.BlockSpec((total_rows, tile), lambda n, s: (0, n)),
            scratch_shapes=[
                pltpu.VMEM((total_rows, width * (height + others)), jnp.bfloat16),
                pltpu.VMEM((total_rows, tile), jnp.float32),
            ],
        ),
        compiler_params=pltpu.CompilerParams(vmem_limit_bytes=VMEM_LIMIT),
        cost_estimate=pl.CostEstimate(
            flops=2 * total_rows * width * (height + others) * columns,
            bytes_accessed=6 * total_rows * columns + 2 * width * (height + others) * columns,
            transcendentals=0,
        ),
        name="last",
    )(scalars, *bases, high, low, high)


def local(tokens, gate_weight, adapter_shrink, adapter_expand, adapter_blocks, adapter_position):
    width = lax.axis_size(AXIS)
    me = lax.axis_index(AXIS)
    shard, depth = tokens.shape
    columns = gate_weight.shape[1]
    rank = adapter_shrink.shape[2]
    total_rows = shard * width
    planes = width // 4
    z, y, core = me // 4, (me // 2) % 2, me % 2

    count = adapter_position.shape[0]
    ids = jnp.arange(count, dtype=jnp.int32)
    capacity = MOST * BLOCK
    starts = jnp.sum(jnp.where(ids[None, :] < ids[:, None], adapter_blocks[None, :], 0), axis=1) * BLOCK
    sizes = adapter_blocks * BLOCK
    at_slot = adapter_position[None, :] == ids[:, None]
    start_by_slot = jnp.sum(jnp.where(at_slot, starts[None, :], 0), axis=1)
    size_by_slot = jnp.sum(jnp.where(at_slot, sizes[None, :], 0), axis=1)
    begin_by_slot = jnp.minimum(start_by_slot, total_rows - capacity)

    def at(z_, y_, core_):
        return (z_ * 2 + y_) * 2 + core_

    both = [(a, b, c) for a in range(planes) for b in range(2) for c in range(2)]
    swap_core = [(at(a, b, c), at(a, b, 1 - c)) for a, b, c in both]
    swap_y = [(at(a, b, c), at(a, 1 - b, c)) for a, b, c in both]
    ring = [0] + list(range(1, planes, 2)) + list(range((planes - 1) // 2 * 2, 0, -2))
    place = [ring.index(a) for a in range(planes)]
    around = [(at(a, b, c), at(ring[(place[a] + 1) % planes], b, c)) for a, b, c in both]
    origin = jnp.asarray([[ring[(place[a] - j) % planes] for j in range(planes)] for a in range(planes)], jnp.int32)
    origin = lax.dynamic_index_in_dim(origin, z, 0, keepdims=False)

    def send(value, pairs):
        return lax.ppermute(value, AXIS, pairs)

    shrink_t = jnp.swapaxes(adapter_shrink[0], 0, 1)
    height = 3 * rank // 4
    spare = -(-(MOST * BLOCK // 2) // (rank - height))

    low, high = parts_of(adapter_expand[0], height, width, spare)
    coming, across = send(tokens, around), send(tokens, swap_y)
    mine, mine_other = tokens, send(tokens, swap_core)
    before, now = [low, high], []
    pieces, places, bases = [], [], []
    some = 2 * planes
    for j in range(planes):
        last_one = j == planes - 1
        if not last_one:
            coming, across = order([coming, across], before)
            onward = send(coming, around) if j + 2 < planes else None
            onward_across = send(coming, swap_y)
            coming_other = send(coming, swap_core)
        else:
            across = order([across], bases)[0]
        across_other = send(across, swap_core)
        before, now = now, [across_other] if last_one else [coming_other, across_other]
        if j + 2 == planes:
            low = order([low], [coming])[0]
            low = lax.all_to_all(low, AXIS, split_axis=0, concat_axis=0, tiled=True)
            arrays = pieces[:some]
            arrays = order(arrays, [coming])
            bases.append(base_matmul(arrays, gate_weight, 4))
        pieces += [mine, across, mine_other, across_other]
        for core_ in (core, 1 - core):
            for y_ in (y, 1 - y):
                places.append(((origin[j] * 2 + y_) * 2 + core_) * shard)
        if not last_one:
            mine, mine_other, coming, across = coming, coming_other, onward, onward_across
    places = jnp.stack(places).astype(jnp.int32)

    mine = jnp.stack([begin_by_slot[me], start_by_slot[me], size_by_slot[me]])
    scalars = jnp.concatenate([places, mine]).astype(jnp.int32)
    high = shrink_rows(scalars, pieces, shrink_t, high, spare)
    high = order([high], [low])[0]
    arrays = order(pieces[some:], [high])
    high = lax.all_to_all(high, AXIS, split_axis=0, concat_axis=0, tiled=True)
    bases.append(base_matmul(arrays, gate_weight))
    scalars = jnp.concatenate([begin_by_slot.astype(jnp.int32), places])
    return last(scalars, bases, low, high, spare, shard)


def solution(mesh):
    return jax.shard_map(
        local,
        mesh=mesh,
        in_specs=(
            P(("groups", "tensor"), None),
            P(None, "tensor"),
            P(("groups", "tensor"), None, None),
            P(("groups", "tensor"), None, None),
            P("groups"),
            P("groups"),
        ),
        out_specs=P("groups", "tensor"),
        check_vma=False,
    )
```
